32 devices in a mesh: dp: 16 (over z, x, core), tensor: 2 (over y).
Axes of the slice: x: 2, y: 2, z: 4, core: 2. Of those that a mesh axis runs over, the one named last changes fastest.
Arguments:
- tokens: bfloat16 [8192, 3072], P('dp', 'tensor'), may hold values from -6 to 6
- hidden_cot: bfloat16 [8192, 8192], P('dp', 'tensor'), may hold values from -1.5 to 1.5
- w_gate: bfloat16 [3072, 8192], P(None, 'tensor'), may hold values from -0.109375 to 0.109375
- w_up: bfloat16 [3072, 8192], P(None, 'tensor'), may hold values from -0.109375 to 0.109375
- expert_ids: int32 [8192, 2], P('dp'), may hold values from 0 to 7, as said below
- route_fixed: int32 [8192, 2], P('dp'), may hold values from 4096 to 65535
Outputs:
- token_grad: bfloat16 [8192, 3072], P('dp', 'tensor')
- gate_grad: bfloat16 [3072, 8192], P('dp', 'tensor')
- up_grad: bfloat16 [3072, 8192], P('dp', 'tensor')
- route_grad: float32 [8192], P('dp')
The draws below stay inside these ranges and needn't reach their ends.
Inputs may be any that keep to these rules, and one draw needn't show every extreme that they name: `expert_ids`: each row names 2 different experts; in each aligned block of 512 rows (the rows of one index of dp), between 128 and 256 rows name expert 0, and exactly 256 in some block.
All inputs are finite; a program needn't handle non-finite values.
Results may differ from the reference program's by a relative error of at most 0.0049.
Values may be sent and summed in bfloat16 or wider, within the bound.
A program may use at most 256 MiB of HBM per device.

```python
import jax
import jax.numpy as jnp
from jax import lax

D = 3072
FF = 8192
EXPERTS = 8
TOP = 2
TOK_DEV = 512
CAP = 256
TOKENS = 8192


def draw_expert_ids(key, part):
    key = jax.random.fold_in(key, 11)
    keys = jax.random.split(key, 6)
    blocks = TOKENS // TOK_DEV
    counts = jax.random.randint(keys[0], (blocks,), CAP // 2, CAP + 1)
    peak = jax.random.randint(keys[1], (), 0, blocks)
    counts = jnp.where(jnp.arange(blocks) == peak, CAP, counts)
    orders = jax.vmap(lambda k: jax.random.permutation(k, TOK_DEV))(jax.random.split(keys[2], blocks))
    ranks = jnp.argsort(orders, axis=1, stable=True).astype(jnp.int32)
    routed = (ranks < counts[:, None]).reshape(TOKENS)
    first = jax.random.randint(keys[3], (TOKENS,), 1, EXPERTS)
    stride = jax.random.randint(keys[4], (TOKENS,), 1, EXPERTS - 1)
    second = 1 + (first - 1 + stride) % (EXPERTS - 1)
    column = jax.random.randint(keys[5], (TOKENS,), 0, 2)
    left = jnp.where(routed, jnp.where(column == 0, 0, first), first)
    right = jnp.where(routed, jnp.where(column == 0, first, 0), second)
    return jnp.stack([left, right], axis=1).astype(jnp.int32)


def with_ends(array, key, least, top_value):
    shape = array.shape
    place = [jax.random.randint(jax.random.fold_in(key, axis), (), 0, shape[axis]) for axis in range(len(shape))]
    array = array.at[tuple(place)].set(least)
    longest = shape.index(max(shape))
    place[longest] = (place[longest] + 1) % shape[longest]
    return array.at[tuple(place)].set(top_value)


def with_spikes(drawn, stream_key, source, target, parts, factor):
    owner, partner = [(jnp.arange(drawn.shape[axis_at]) // (drawn.shape[axis_at] // parts)).reshape([-1 if axis == axis_at else 1 for axis in range(drawn.ndim)]) for axis_at in (source, target)]
    chosen = jax.random.permutation(stream_key, parts)[partner]
    strong = (owner == chosen) | (owner == (partner + parts // 2) % parts)
    return jnp.where(strong, factor * drawn, drawn)


def level_of(rng, shape, shards, least, largest):
    loudness, own = 1.0, jax.random.fold_in(rng, 6)
    for position, shards_of in shards:
        steps = jnp.exp(jax.random.uniform(jax.random.fold_in(own, position), (shards_of,), jnp.float32, least / len(shards), largest / len(shards)))
        loudness = loudness * jnp.repeat(steps, shape[position] // shards_of).reshape([-1 if axis == position else 1 for axis in range(len(shape))])
    return loudness


def centred(key, extent, width, bound, pieces=(), dtype=jnp.bfloat16):
    result = width * jax.random.normal(key, extent, jnp.float32)
    if pieces:
        result = result * level_of(key, extent, pieces, -0.22, 0.18)
    return jnp.clip(result, -bound, bound).astype(dtype)


def heavy_noise(key, extent, scale, limit, shards, heavy, kind=jnp.bfloat16):
    array = scale * jax.random.normal(key, extent, jnp.float32)
    if shards:
        array = array * level_of(key, extent, shards, -0.22, 0.18)
    return jnp.clip(with_spikes(array, jax.random.fold_in(key, 3), *heavy), -limit, limit).astype(kind)


def setup_inputs(seed: int = 0) -> dict:
    arg_keys = jax.random.split(jax.random.key(seed), 7)
    return {
        "tokens": heavy_noise(arg_keys[0], (TOKENS, D), 1.0, 6.0, ((0, 16), (1, 2)), (0, 1, 16, 2.0)),
        "hidden_cot": centred(arg_keys[1], (TOKENS, FF), 0.25, 1.5, ((0, 16), (1, 2))),
        "w_gate": centred(arg_keys[2], (D, FF), D ** -0.5, 0.109375, ((1, 2),)),
        "w_up": centred(arg_keys[3], (D, FF), D ** -0.5, 0.109375, ((1, 2),)),
        "expert_ids": draw_expert_ids(jax.random.fold_in(arg_keys[6], 71), 0),
        "route_fixed": with_ends(jax.random.randint(arg_keys[5], (TOKENS, TOP), 4096, 65536), jax.random.fold_in(arg_keys[5], 1), 4096, 65535).astype(jnp.int32),
    }


def reference(tokens, hidden_cot, w_gate, w_up, expert_ids, route_fixed):
    gate_pre = jnp.dot(tokens, w_gate, preferred_element_type=jnp.float32)
    up_pre = jnp.dot(tokens, w_up, preferred_element_type=jnp.float32)
    selected = expert_ids == 0
    routed = jnp.any(selected, axis=1).astype(jnp.float32)
    share = jnp.sum(jnp.where(selected, route_fixed, 0), axis=1).astype(jnp.float32) / 65536.0
    sigmoid_gate = jax.nn.sigmoid(gate_pre)
    activated = gate_pre * sigmoid_gate
    hidden = (activated * up_pre).astype(jnp.bfloat16)
    hidden = lax.optimization_barrier(hidden)
    hidden_wide = hidden.astype(jnp.float32)
    cot_wide = hidden_cot.astype(jnp.float32)
    route_grad = routed * jnp.sum(hidden_wide * cot_wide, axis=1)
    scaled = share[:, None] * cot_wide
    gate_cot = (scaled * up_pre * sigmoid_gate * (1.0 + gate_pre * (1.0 - sigmoid_gate))).astype(jnp.bfloat16)
    up_cot = (scaled * activated).astype(jnp.bfloat16)
    dims = (((1,), (1,)), ((), ()))
    token_grad = lax.dot_general(gate_cot, w_gate, dims, preferred_element_type=jnp.float32)
    token_grad = token_grad + lax.dot_general(up_cot, w_up, dims, preferred_element_type=jnp.float32)
    rows_dims = (((0,), (0,)), ((), ()))
    gate_grad = lax.dot_general(tokens, gate_cot, rows_dims, preferred_element_type=jnp.float32)
    up_grad = lax.dot_general(tokens, up_cot, rows_dims, preferred_element_type=jnp.float32)
    return (token_grad.astype(jnp.bfloat16), gate_grad.astype(jnp.bfloat16), up_grad.astype(jnp.bfloat16), route_grad)
```

```python
import functools

import jax
import jax.numpy as jnp
from jax import lax
from jax.sharding import PartitionSpec as P

CAP = 256
CHUNKS = 4


def on_device(ndp, ntp, tokens, hidden_cot, w_gate, w_up, expert_ids, route_fixed):
    n_high = ndp // 8
    me = lax.axis_index("dp")
    core, x_at, z_low, z_high = me % 2, (me // 2) % 2, (me // 4) % 2, me // 8
    tensor_at = lax.axis_index("tensor")
    is_gate = core == 0

    def flip(value, bit):
        return lax.ppermute(value, "dp", [(i, i ^ bit) for i in range(ndp)])

    def shift_high(value, step):
        return lax.ppermute(value, "dp", [(i, (i + 8 * step) % ndp) for i in range(ndp)])

    def shift_tensor(value, step):
        return lax.ppermute(value, "tensor", [(i, (i + step) % ntp) for i in range(ntp)])

    selected = expert_ids == 0
    routed_flag = jnp.any(selected, axis=1)
    slot_of = jnp.cumsum(routed_flag.astype(jnp.int32)) - 1
    slot_ids = jnp.arange(CAP, dtype=jnp.int32)
    dispatch_mask = (slot_of[None, :] == slot_ids[:, None]) & routed_flag[None, :]
    dispatch = dispatch_mask.astype(jnp.bfloat16)
    dispatch_wide = dispatch_mask.astype(jnp.float32)
    share_all = jnp.sum(jnp.where(selected, route_fixed, 0), axis=1).astype(jnp.float32) / 65536.0
    share = jnp.dot(dispatch_wide, share_all, precision=lax.Precision.HIGHEST)
    routed = jnp.sum(dispatch_wide, axis=1)
    picked = jnp.dot(dispatch, tokens, preferred_element_type=jnp.float32).astype(jnp.bfloat16)
    gathered = lax.all_gather(picked, "tensor", axis=1, tiled=True)
    cot_rows = jnp.dot(dispatch, hidden_cot, preferred_element_type=jnp.float32).astype(
        jnp.bfloat16
    )

    depth = gathered.shape[1] // ndp
    features = gathered.reshape(CAP, n_high, 2, 2, 2 * depth)
    near = lax.dynamic_index_in_dim(features, z_low, 2, keepdims=False)
    far = flip(lax.dynamic_index_in_dim(features, 1 - z_low, 2, keepdims=False), 4)
    both = jnp.stack([near, far])
    here = lax.dynamic_index_in_dim(both, x_at, 3, keepdims=False)
    there = flip(lax.dynamic_index_in_dim(both, 1 - x_at, 3, keepdims=False), 2)
    mine = jnp.concatenate([here, there])
    group = jnp.stack([mine, flip(mine, 1)], axis=1)
    group = group.reshape(8 * CAP, n_high, 2 * depth)
    group_of = [
        lax.dynamic_index_in_dim(group, (z_high + s) % n_high, 1, keepdims=False)
        for s in range(n_high)
    ]

    width = w_gate.shape[1]
    step = width // CHUNKS
    route_sum = jnp.zeros((CAP,), jnp.float32)
    gate_cots, up_cots, gates, ups = [], [], [], []
    rows_dims = (((0,), (0,)), ((), ()))
    for chunk in range(CHUNKS):
        columns = slice(chunk * step, (chunk + 1) * step)
        gate_pre = jnp.dot(gathered, w_gate[:, columns], preferred_element_type=jnp.float32)
        up_pre = jnp.dot(gathered, w_up[:, columns], preferred_element_type=jnp.float32)
        sigmoid_gate = jax.nn.sigmoid(gate_pre)
        activated = gate_pre * sigmoid_gate
        hidden = (activated * up_pre).astype(jnp.bfloat16)
        hidden = lax.optimization_barrier(hidden)
        cot_wide = cot_rows[:, columns].astype(jnp.float32)
        route_sum += jnp.sum(hidden.astype(jnp.float32) * cot_wide, axis=1)
        scaled = share[:, None] * cot_wide
        gate_cot = (
            scaled * up_pre * sigmoid_gate * (1.0 + gate_pre * (1.0 - sigmoid_gate))
        ).astype(jnp.bfloat16)
        up_cot = (scaled * activated).astype(jnp.bfloat16)
        gate_cots.append(gate_cot)
        up_cots.append(up_cot)
        kept = jnp.where(is_gate, gate_cot, up_cot)
        pair = jnp.concatenate([kept, flip(jnp.where(is_gate, up_cot, gate_cot), 1)])
        z_pair = flip(pair, 4)
        x_pair = flip(pair, 2)
        xz_pair = flip(z_pair, 2)
        cots = jnp.concatenate([pair, z_pair, x_pair, xz_pair])
        arrived = []
        for s in range(1, n_high):
            partial = lax.dot_general(
                group_of[s], cots, rows_dims, preferred_element_type=jnp.float32
            ).astype(jnp.bfloat16)
            arrived.append(shift_high(partial, s))
        total = lax.dot_general(group_of[0], cots, rows_dims, preferred_element_type=jnp.float32)
        for term in arrived:
            total += term.astype(jnp.float32)
        total = total.astype(jnp.bfloat16).reshape(2, depth, step)
        own = lax.dynamic_index_in_dim(total, core, 0, keepdims=False)
        other = flip(lax.dynamic_index_in_dim(total, 1 - core, 0, keepdims=False), 1)
        gates.append(jnp.where(is_gate, own, other))
        ups.append(jnp.where(is_gate, other, own))
    gate_grad = jnp.concatenate(gates, axis=1)
    up_grad = jnp.concatenate(ups, axis=1)

    slot_route = route_sum
    for s in range(1, ntp):
        slot_route += shift_tensor(route_sum, s)
    route_grad = jnp.dot(routed * slot_route, dispatch_wide, precision=lax.Precision.HIGHEST)

    dims = (((1,), (1,)), ((), ()))
    transposed = lax.dot_general(
        w_gate, jnp.concatenate(gate_cots, axis=1), dims, preferred_element_type=jnp.float32
    )
    transposed += lax.dot_general(
        w_up, jnp.concatenate(up_cots, axis=1), dims, preferred_element_type=jnp.float32
    )
    blocks = transposed.reshape(ntp, -1, CAP)
    slot_grad = lax.dynamic_index_in_dim(blocks, tensor_at, 0, keepdims=False)
    for s in range(1, ntp):
        to = lax.dynamic_index_in_dim(blocks, (tensor_at + s) % ntp, 0, keepdims=False)
        slot_grad += shift_tensor(to, s)
    back_dims = (((0,), (0,)), ((), ()))
    token_grad = lax.dot_general(
        dispatch,
        slot_grad.T.astype(jnp.bfloat16),
        back_dims,
        preferred_element_type=jnp.float32,
    ).astype(jnp.bfloat16)
    return token_grad, gate_grad, up_grad, route_grad


def solution(mesh):
    return jax.shard_map(
        functools.partial(on_device, mesh.shape["dp"], mesh.shape["tensor"]),
        mesh=mesh,
        in_specs=(
            P("dp", "tensor"),
            P("dp", "tensor"),
            P(None, "tensor"),
            P(None, "tensor"),
            P("dp", None),
            P("dp", None),
        ),
        out_specs=(P("dp", "tensor"), P("dp", "tensor"), P("dp", "tensor"), P("dp")),
        check_vma=False,
    )
```

```python
import functools

import jax
import jax.numpy as jnp
from jax import lax
from jax.sharding import PartitionSpec as P

CAP = 256
CHUNKS = 8
SPLIT = 2


def on_device(ndp, ntp, tokens, hidden_cot, w_gate, w_up, expert_ids, route_fixed):
    n_high = ndp // 8
    me = lax.axis_index("dp")
    core, x_at, z_low, z_high = me % 2, (me // 2) % 2, (me // 4) % 2, me // 8
    tensor_at = lax.axis_index("tensor")
    is_gate = core == 0

    def flip(value, bit):
        return lax.ppermute(value, "dp", [(i, i ^ bit) for i in range(ndp)])

    def shift_high(value, step):
        return lax.ppermute(value, "dp", [(i, (i + 8 * step) % ndp) for i in range(ndp)])

    def shift_tensor(value, step):
        return lax.ppermute(value, "tensor", [(i, (i + step) % ntp) for i in range(ntp)])

    selected = expert_ids == 0
    routed_flag = jnp.any(selected, axis=1)
    slot_of = jnp.cumsum(routed_flag.astype(jnp.int32)) - 1
    slot_ids = jnp.arange(CAP, dtype=jnp.int32)
    dispatch_mask = (slot_of[None, :] == slot_ids[:, None]) & routed_flag[None, :]
    dispatch = dispatch_mask.astype(jnp.bfloat16)
    dispatch_wide = dispatch_mask.astype(jnp.float32)
    share_all = jnp.sum(jnp.where(selected, route_fixed, 0), axis=1).astype(jnp.float32) / 65536.0
    share = jnp.dot(dispatch_wide, share_all, precision=lax.Precision.HIGHEST)
    routed = jnp.sum(dispatch_wide, axis=1)
    picked = jnp.dot(dispatch, tokens, preferred_element_type=jnp.float32).astype(jnp.bfloat16)
    parts = lax.dynamic_update_index_in_dim(
        jnp.zeros((CAP, ntp, picked.shape[1]), jnp.bfloat16), picked, tensor_at, 1
    )
    for s in range(1, ntp):
        parts = lax.dynamic_update_index_in_dim(
            parts, shift_tensor(picked, s), (tensor_at + ntp - s) % ntp, 1
        )
    gathered = parts.reshape(CAP, -1)
    cot_rows = jnp.dot(dispatch, hidden_cot, preferred_element_type=jnp.float32).astype(
        jnp.bfloat16
    )

    depth = gathered.shape[1] // ndp
    features = gathered.reshape(CAP, n_high, 2, 2, 2 * depth)
    near = lax.dynamic_index_in_dim(features, z_low, 2, keepdims=False)
    far = flip(lax.dynamic_index_in_dim(features, 1 - z_low, 2, keepdims=False), 4)
    both = jnp.stack([near, far])
    here = lax.dynamic_index_in_dim(both, x_at, 3, keepdims=False)
    there = flip(lax.dynamic_index_in_dim(both, 1 - x_at, 3, keepdims=False), 2)
    mine = jnp.concatenate([here, there])
    group = jnp.stack([mine, flip(mine, 1)], axis=1)
    group = group.reshape(8 * CAP, n_high, 2 * depth)

    width = w_gate.shape[1]
    step = width // CHUNKS
    rows_dims = (((0,), (0,)), ((), ()))
    dims = (((1,), (1,)), ((), ()))

    def cotangents(rows, chunk):
        columns = slice(chunk * step * SPLIT, (chunk + 1) * step * SPLIT)
        gate_pre = jnp.dot(rows, w_gate[:, columns], preferred_element_type=jnp.float32)
        up_pre = jnp.dot(rows, w_up[:, columns], preferred_element_type=jnp.float32)
        sigmoid_gate = jax.nn.sigmoid(gate_pre)
        activated = gate_pre * sigmoid_gate
        hidden = (activated * up_pre).astype(jnp.bfloat16)
        hidden = lax.optimization_barrier(hidden)
        cot_wide = cot_rows[:, columns].astype(jnp.float32)
        route = jnp.sum(hidden.astype(jnp.float32) * cot_wide, axis=1)
        scaled = share[:, None] * cot_wide
        gate_cot = (
            scaled * up_pre * sigmoid_gate * (1.0 + gate_pre * (1.0 - sigmoid_gate))
        ).astype(jnp.bfloat16)
        up_cot = (scaled * activated).astype(jnp.bfloat16)
        return gate_cot, up_cot, route

    tie = lambda *values: lax.optimization_barrier(values)
    gate_cots, up_cots, routes = [], [], []
    pairs, z_pairs, x_pairs, firsts, sent, totals = [], [], [], [], [], []

    def finish(j):
        xz_pair = flip(z_pairs[j], 2)
        cots = jnp.concatenate([pairs[j], z_pairs[j], x_pairs[j], xz_pair])
        partials = [
            lax.dot_general(
                group_of[s], cots, rows_dims, preferred_element_type=jnp.float32
            ).astype(jnp.bfloat16)
            for s in range(1, n_high)
        ]
        sent.append(partials)
        totals.append(
            lax.dot_general(group_of[0], cots, rows_dims, preferred_element_type=jnp.float32)
        )

    rows = gathered
    for j in range(CHUNKS):
        if j % SPLIT == 0:
            if j == SPLIT:
                rows, pairs[0] = tie(rows, pairs[0])
            if j > SPLIT:
                rows, x_pairs[j - 2 * SPLIT] = tie(rows, x_pairs[j - 2 * SPLIT])
            gate_wide, up_wide, route = cotangents(rows, j // SPLIT)
            gate_cots.append(gate_wide)
            up_cots.append(up_wide)
            routes.append(route)
        part = slice(j % SPLIT * step, (j % SPLIT + 1) * step)
        gate_cot, up_cot = gate_wide[:, part], up_wide[:, part]
        kept = jnp.where(is_gate, gate_cot, up_cot)
        passed = jnp.where(is_gate, up_cot, gate_cot)
        if j == 0:
            passed, group = tie(passed, group)
            group_of = [
                lax.dynamic_index_in_dim(group, (z_high + s) % n_high, 1, keepdims=False)
                for s in range(n_high)
            ]
        pair = jnp.concatenate([kept, flip(passed, 1)])
        if j >= 2:
            pair, z_pairs[j - 2], x_pairs[j - 2] = tie(pair, z_pairs[j - 2], x_pairs[j - 2])
            finish(j - 2)
        if j >= 4:
            pair, *sent[j - 4] = tie(pair, *sent[j - 4])
        pairs.append(pair)
        z_pairs.append(flip(pair, 4))
        x_pairs.append(flip(pair, 2))
    finish(CHUNKS - 2)
    finish(CHUNKS - 1)

    gates, ups = [], []
    for j in range(CHUNKS):
        total = totals[j]
        for s in range(1, n_high):
            total += shift_high(sent[j][s - 1], s).astype(jnp.float32)
        total = total.astype(jnp.bfloat16).reshape(2, depth, step)
        own = lax.dynamic_index_in_dim(total, core, 0, keepdims=False)
        other = flip(lax.dynamic_index_in_dim(total, 1 - core, 0, keepdims=False), 1)
        gates.append(jnp.where(is_gate, own, other))
        ups.append(jnp.where(is_gate, other, own))
    gate_grad = jnp.concatenate(gates, axis=1)
    up_grad = jnp.concatenate(ups, axis=1)
    route_sum = sum(routes)

    slot_route = route_sum
    for s in range(1, ntp):
        slot_route += shift_tensor(route_sum, s)
    route_grad = jnp.dot(routed * slot_route, dispatch_wide, precision=lax.Precision.HIGHEST)

    transposed = lax.dot_general(
        w_gate, jnp.concatenate(gate_cots, axis=1), dims, preferred_element_type=jnp.float32
    )
    transposed += lax.dot_general(
        w_up, jnp.concatenate(up_cots, axis=1), dims, preferred_element_type=jnp.float32
    )
    blocks = transposed.reshape(ntp, -1, CAP)
    slot_grad = lax.dynamic_index_in_dim(blocks, tensor_at, 0, keepdims=False)
    for s in range(1, ntp):
        to = lax.dynamic_index_in_dim(blocks, (tensor_at + s) % ntp, 0, keepdims=False)
        slot_grad += shift_tensor(to, s)
    back_dims = (((0,), (0,)), ((), ()))
    token_grad = lax.dot_general(
        dispatch,
        slot_grad.T.astype(jnp.bfloat16),
        back_dims,
        preferred_element_type=jnp.float32,
    ).astype(jnp.bfloat16)
    return token_grad, gate_grad, up_grad, route_grad


def solution(mesh):
    return jax.shard_map(
        functools.partial(on_device, mesh.shape["dp"], mesh.shape["tensor"]),
        mesh=mesh,
        in_specs=(
            P("dp", "tensor"),
            P("dp", "tensor"),
            P(None, "tensor"),
            P(None, "tensor"),
            P("dp", None),
            P("dp", None),
        ),
        out_specs=(P("dp", "tensor"), P("dp", "tensor"), P("dp", "tensor"), P("dp")),
        check_vma=False,
    )
```

```python
import functools

import jax
import jax.numpy as jnp
from jax import lax
from jax.sharding import PartitionSpec as P

CAP = 256
CHUNKS = 8
SPLIT = 2


def on_device(ndp, ntp, tokens, hidden_cot, w_gate, w_up, expert_ids, route_fixed):
    n_high = ndp // 8
    me = lax.axis_index("dp")
    core, x_at, z_low, z_high = me % 2, (me // 2) % 2, (me // 4) % 2, me // 8
    tensor_at = lax.axis_index("tensor")
    is_gate = core == 0

    def flip(value, bit):
        return lax.ppermute(value, "dp", [(i, i ^ bit) for i in range(ndp)])

    def shift_high(value, step):
        return lax.ppermute(value, "dp", [(i, (i + 8 * step) % ndp) for i in range(ndp)])

    def shift_tensor(value, step):
        return lax.ppermute(value, "tensor", [(i, (i + step) % ntp) for i in range(ntp)])

    selected = expert_ids == 0
    routed_flag = jnp.any(selected, axis=1)
    slot_of = jnp.cumsum(routed_flag.astype(jnp.int32)) - 1
    slot_ids = jnp.arange(CAP, dtype=jnp.int32)
    dispatch_mask = (slot_of[None, :] == slot_ids[:, None]) & routed_flag[None, :]
    dispatch = dispatch_mask.astype(jnp.bfloat16)
    dispatch_wide = dispatch_mask.astype(jnp.float32)
    share_all = jnp.sum(jnp.where(selected, route_fixed, 0), axis=1).astype(jnp.float32) / 65536.0
    share = jnp.dot(dispatch_wide, share_all, precision=lax.Precision.HIGHEST)
    routed = jnp.sum(dispatch_wide, axis=1)
    picked = jnp.dot(dispatch, tokens, preferred_element_type=jnp.float32).astype(jnp.bfloat16)
    parts = lax.dynamic_update_index_in_dim(
        jnp.zeros((CAP, ntp, picked.shape[1]), jnp.bfloat16), picked, tensor_at, 1
    )
    for s in range(1, ntp):
        parts = lax.dynamic_update_index_in_dim(
            parts, shift_tensor(picked, s), (tensor_at + ntp - s) % ntp, 1
        )
    gathered = parts.reshape(CAP, -1)
    cot_rows = jnp.dot(dispatch, hidden_cot, preferred_element_type=jnp.float32).astype(
        jnp.bfloat16
    )

    depth = gathered.shape[1] // ndp
    features = gathered.reshape(CAP, n_high, 2, 2, 2 * depth)
    near = lax.dynamic_index_in_dim(features, z_low, 2, keepdims=False)
    far = flip(lax.dynamic_index_in_dim(features, 1 - z_low, 2, keepdims=False), 4)
    width = w_gate.shape[1]
    step = width // CHUNKS
    rows_dims = (((0,), (0,)), ((), ()))
    dims = (((1,), (1,)), ((), ()))

    def cotangents(rows, chunk):
        columns = slice(chunk * step * SPLIT, (chunk + 1) * step * SPLIT)
        gate_pre = jnp.dot(rows, w_gate[:, columns], preferred_element_type=jnp.float32)
        up_pre = jnp.dot(rows, w_up[:, columns], preferred_element_type=jnp.float32)
        sigmoid_gate = jax.nn.sigmoid(gate_pre)
        activated = gate_pre * sigmoid_gate
        hidden = (activated * up_pre).astype(jnp.bfloat16)
        hidden = lax.optimization_barrier(hidden)
        cot_wide = cot_rows[:, columns].astype(jnp.float32)
        route = jnp.sum(hidden.astype(jnp.float32) * cot_wide, axis=1)
        scaled = share[:, None] * cot_wide
        gate_cot = (
            scaled * up_pre * sigmoid_gate * (1.0 + gate_pre * (1.0 - sigmoid_gate))
        ).astype(jnp.bfloat16)
        up_cot = (scaled * activated).astype(jnp.bfloat16)
        return gate_cot, up_cot, route

    tie = lambda *values: lax.optimization_barrier(values)
    gate_cots, up_cots, routes = [], [], []
    pairs, z_pairs, x_pairs, xz_pairs, sent, totals = [], [], [], [], [], []

    def finish(j):
        xz_pair = flip(z_pairs[j], 2)
        xz_pairs.append(xz_pair)
        cots = jnp.concatenate([pairs[j], z_pairs[j], x_pairs[j], xz_pair])
        partials = [
            lax.dot_general(
                group_of[s], cots, rows_dims, preferred_element_type=jnp.float32
            ).astype(jnp.bfloat16)
            for s in range(1, n_high)
        ]
        sent.append(partials)
        totals.append(
            lax.dot_general(group_of[0], cots, rows_dims, preferred_element_type=jnp.float32)
        )

    def add_grad(grad, k):
        columns = slice(k * step * SPLIT, (k + 1) * step * SPLIT)
        for weight, cot in ((w_gate, gate_cots[k]), (w_up, up_cots[k])):
            term = lax.dot_general(
                weight[:, columns], cot, dims, preferred_element_type=jnp.float32
            )
            grad = term if grad is None else grad + term
        return grad

    rows = gathered
    grad = None
    for j in range(CHUNKS):
        if j % SPLIT == 0:
            if j == SPLIT:
                rows, pairs[1] = tie(rows, pairs[1])
            if j > SPLIT:
                rows, x_pairs[j - 3] = tie(rows, x_pairs[j - 3])
            gate_wide, up_wide, route = cotangents(rows, j // SPLIT)
            gate_cots.append(gate_wide)
            up_cots.append(up_wide)
            routes.append(route)
        part = slice(j % SPLIT * step, (j % SPLIT + 1) * step)
        gate_cot, up_cot = gate_wide[:, part], up_wide[:, part]
        kept = jnp.where(is_gate, gate_cot, up_cot)
        passed = jnp.where(is_gate, up_cot, gate_cot)
        pair = jnp.concatenate([kept, flip(passed, 1)])
        if j == 1:
            pair, far = tie(pair, far)
            both = jnp.stack([near, far])
            here = lax.dynamic_index_in_dim(both, x_at, 3, keepdims=False)
            there = flip(lax.dynamic_index_in_dim(both, 1 - x_at, 3, keepdims=False), 2)
        if j == 3:
            pair, there = tie(pair, there)
            mine = jnp.concatenate([here, there])
            group = jnp.stack([mine, flip(mine, 1)], axis=1)
            group = group.reshape(8 * CAP, n_high, 2 * depth)
            group_of = [
                lax.dynamic_index_in_dim(group, (z_high + s) % n_high, 1, keepdims=False)
                for s in range(n_high)
            ]
            finish(0)
        if j == 5 or j == 7:
            grad = add_grad(grad, j // 2 - 2)
            pair, grad = tie(pair, grad)
        if j >= 2:
            pair, z_pairs[j - 2], x_pairs[j - 2] = tie(pair, z_pairs[j - 2], x_pairs[j - 2])
            if j > 2:
                finish(j - 2)
        if j >= 4:
            pair, *sent[j - 4] = tie(pair, *sent[j - 4])
        if j == 4 or j == 6:
            k = j // 2 - 2
            pair, gate_cots[k], up_cots[k] = tie(pair, gate_cots[k], up_cots[k])
        if j == 7:
            pair, *late = tie(pair, *gate_cots[2:], *up_cots[2:])
            gate_cots[2:], up_cots[2:] = late[:2], late[2:]
        pairs.append(pair)
        z_pairs.append(flip(pair, 4))
        x_pairs.append(flip(pair, 2))
    finish(CHUNKS - 2)
    grad = add_grad(add_grad(grad, 2), 3)
    z_pairs[-1], grad = tie(z_pairs[-1], grad)
    finish(CHUNKS - 1)

    gates, ups = [], []
    for j in range(CHUNKS):
        terms = [shift_high(sent[j][s - 1], s) for s in range(1, n_high)]
        if j < CHUNKS - 4:
            *terms, xz_pairs[j + 4] = tie(*terms, xz_pairs[j + 4])
        elif j < CHUNKS - 1:
            *terms, totals[-1] = tie(*terms, totals[-1])
        total = totals[j]
        for term in terms:
            total += term.astype(jnp.float32)
        total = total.astype(jnp.bfloat16).reshape(2, depth, step)
        own = lax.dynamic_index_in_dim(total, core, 0, keepdims=False)
        other = flip(lax.dynamic_index_in_dim(total, 1 - core, 0, keepdims=False), 1)
        gates.append(jnp.where(is_gate, own, other))
        ups.append(jnp.where(is_gate, other, own))
    gate_grad = jnp.concatenate(gates, axis=1)
    up_grad = jnp.concatenate(ups, axis=1)
    route_sum = sum(routes)

    slot_route = route_sum
    for s in range(1, ntp):
        slot_route += shift_tensor(route_sum, s)
    route_grad = jnp.dot(routed * slot_route, dispatch_wide, precision=lax.Precision.HIGHEST)

    blocks = grad.reshape(ntp, -1, CAP)
    slot_grad = lax.dynamic_index_in_dim(blocks, tensor_at, 0, keepdims=False)
    for s in range(1, ntp):
        to = lax.dynamic_index_in_dim(blocks, (tensor_at + s) % ntp, 0, keepdims=False)
        slot_grad += shift_tensor(to, s)
    back_dims = (((0,), (0,)), ((), ()))
    token_grad = lax.dot_general(
        dispatch,
        slot_grad.T.astype(jnp.bfloat16),
        back_dims,
        preferred_element_type=jnp.float32,
    ).astype(jnp.bfloat16)
    return token_grad, gate_grad, up_grad, route_grad


def solution(mesh):
    return jax.shard_map(
        functools.partial(on_device, mesh.shape["dp"], mesh.shape["tensor"]),
        mesh=mesh,
        in_specs=(
            P("dp", "tensor"),
            P("dp", "tensor"),
            P(None, "tensor"),
            P(None, "tensor"),
            P("dp", None),
            P("dp", None),
        ),
        out_specs=(P("dp", "tensor"), P("dp", "tensor"), P("dp", "tensor"), P("dp")),
        check_vma=False,
    )
```

```python
import functools

import jax
import jax.numpy as jnp
from jax import lax
from jax.experimental import pallas as pl
from jax.experimental.pallas import tpu as pltpu
from jax.sharding import PartitionSpec as P

CAP = 256
CHUNKS = 8
WIDE = 4
MESH = pl.DeviceIdType.MESH


def exchange(ndp, ntp, kept, passed, feats, w_gate, w_up, own_out, other_out, slot_out,
             cots, partial, landed, summed, swapped, weights, grad, grad_in,
             send, recv, high_send, high_recv, y_send, y_recv, weight_sem):
    n_high = ndp // 8
    me = lax.axis_index("dp")
    at = lax.axis_index("tensor")
    core, high = me % 2, me // 8
    core_peer = me + 1 - 2 * core
    x_peer = me + 2 - 4 * ((me // 2) % 2)
    z_peer = me + 4 - 8 * ((me // 4) % 2)
    highs = [((high + s) % n_high) * 8 + me % 8 for s in range(1, n_high)]
    tensors = [(at + s) % ntp for s in range(1, ntp)]
    slots, step = kept.shape[1], kept.shape[2]
    depth = own_out.shape[1]
    block = slot_out.shape[0]
    tile = min(block, 512)

    barrier = pltpu.get_barrier_semaphore()
    for peer in [core_peer, x_peer, z_peer] + highs:
        pl.semaphore_signal(barrier, inc=1, device_id=(peer, at), device_id_type=MESH)
    for peer in tensors:
        pl.semaphore_signal(barrier, inc=1, device_id=(me, peer), device_id_type=MESH)
    pl.semaphore_wait(barrier, 3 + len(highs) + len(tensors))

    def remote(src, dst, send_sem, recv_sem, device):
        return pltpu.make_async_remote_copy(
            src_ref=src, dst_ref=dst, send_sem=send_sem, recv_sem=recv_sem,
            device_id=device, device_id_type=MESH,
        )

    def rows(j, which, count=2):
        return cots.at[j, pl.ds(which * slots, count * slots)]

    def to_core(j):
        return remote(passed.at[j], rows(j, 1, 1), send.at[0, j], recv.at[0, j], (core_peer, at))

    def to_z(j):
        return remote(rows(j, 0), rows(j, 2), send.at[1, j], recv.at[1, j], (z_peer, at))

    def to_x(j):
        return remote(rows(j, 0), rows(j, 4), send.at[2, j], recv.at[2, j], (x_peer, at))

    def on_to_x(j):
        return remote(rows(j, 2), rows(j, 6), send.at[3, j], recv.at[3, j], (x_peer, at))

    def swap(j):
        return remote(
            summed.at[j, 1 - core], swapped.at[j], send.at[4, j], recv.at[4, j], (core_peer, at)
        )

    def to_high(j, s):
        return remote(
            partial.at[s, j], landed.at[s, j], high_send.at[s, j], high_recv.at[s, j],
            (highs[s], at),
        )

    def to_tensor(s):
        start = pl.multiple_of(tensors[s] * block, block)
        return remote(
            grad.at[pl.ds(start, block)], grad_in.at[s], y_send.at[s], y_recv.at[s],
            (me, tensors[s]),
        )

    def weight_copy(i, source):
        columns = pl.ds((i // 2) * step, step)
        return pltpu.make_async_copy(
            source.at[:, columns], weights.at[i % 2], weight_sem.at[i % 2]
        )

    def fetch(i):
        takes_gate = core == i % 2

        @pl.when(takes_gate)
        def _():
            weight_copy(i, w_gate).start()

        @pl.when(jnp.logical_not(takes_gate))
        def _():
            weight_copy(i, w_up).start()

    def grad_turn(i):
        weight_copy(i, w_gate).wait()
        cot = (kept if i % 2 == 0 else passed).at[i // 2]

        def body(k, carry):
            part = pl.ds(pl.multiple_of(k * tile, tile), tile)
            term = lax.dot_general(
                weights[i % 2, part, :], cot[...], (((1,), (1,)), ((), ())),
                preferred_element_type=jnp.float32,
            )
            grad[part, :] = term if i == 0 else grad[part, :] + term
            return carry

        lax.fori_loop(0, grad.shape[0] // tile, body, 0)
        if i + 2 < 2 * CHUNKS:
            fetch(i + 2)

    def multiply(j, s, half):
        return jnp.dot(feats[s, half], cots[j], preferred_element_type=jnp.float32)

    def send_sums(j):
        for s in range(n_high - 1):
            def body(half, carry):
                partial[s, j, half] = multiply(j, s + 1, half).astype(jnp.bfloat16)
                return carry

            lax.fori_loop(0, 2, body, 0)
            to_high(j, s).start()

    def finish(j):
        for s in range(n_high - 1):
            to_high(j, s).wait_recv()

        def body(half, carry):
            total = multiply(j, 0, half)
            for s in range(n_high - 1):
                total += landed[s, j, half].astype(jnp.float32)
            summed[j, half] = total.astype(jnp.bfloat16)
            return carry

        lax.fori_loop(0, 2, body, 0)
        swap(j).start()
        own_out[j] = summed[j, core]

    fetch(0)
    fetch(1)
    for j in range(CHUNKS):
        to_core(j).start()
    for j in range(CHUNKS):
        cots[j, 0:slots] = kept[j]
    for t in range(CHUNKS + 2):
        if t < CHUNKS:
            to_core(t).wait_recv()
            to_z(t).start()
            to_x(t).start()
        if 1 <= t <= CHUNKS:
            to_z(t - 1).wait_recv()
            on_to_x(t - 1).start()
        if t < CHUNKS:
            grad_turn(2 * t)
            grad_turn(2 * t + 1)
        if t == CHUNKS - 1:
            for s in range(ntp - 1):
                to_tensor(s).start()
        if t >= 2:
            to_x(t - 2).wait_recv()
            on_to_x(t - 2).wait_recv()
            send_sums(t - 2)
        if t >= 4:
            finish(t - 4)
    for s in range(ntp - 1):
        to_tensor(s).wait_recv()
    here = pl.ds(pl.multiple_of(at * block, block), block)
    slot = grad[here, :]
    for s in range(ntp - 1):
        slot += grad_in[s]
    slot_out[...] = slot
    for j in range(CHUNKS - 2, CHUNKS):
        finish(j)
    for j in range(CHUNKS):
        swap(j).wait_recv()
        other_out[j] = swapped[j]
        for copy in (to_core(j), to_z(j), to_x(j), on_to_x(j), swap(j)):
            copy.wait_send()
        for s in range(n_high - 1):
            to_high(j, s).wait_send()
    for s in range(ntp - 1):
        to_tensor(s).wait_send()


def on_device(ndp, ntp, tokens, hidden_cot, w_gate, w_up, expert_ids, route_fixed):
    n_high = ndp // 8
    me = lax.axis_index("dp")
    core, x_at, z_low, z_high = me % 2, (me // 2) % 2, (me // 4) % 2, me // 8
    tensor_at = lax.axis_index("tensor")
    is_gate = core == 0

    def flip(value, bit):
        return lax.ppermute(value, "dp", [(i, i ^ bit) for i in range(ndp)])

    def shift_high(value, step):
        return lax.ppermute(value, "dp", [(i, (i + 8 * step) % ndp) for i in range(ndp)])

    def shift_tensor(value, step):
        return lax.ppermute(value, "tensor", [(i, (i + step) % ntp) for i in range(ntp)])

    selected = expert_ids == 0
    routed_flag = jnp.any(selected, axis=1)
    slot_of = jnp.cumsum(routed_flag.astype(jnp.int32)) - 1
    slot_ids = jnp.arange(CAP, dtype=jnp.int32)
    dispatch_mask = (slot_of[None, :] == slot_ids[:, None]) & routed_flag[None, :]
    dispatch = dispatch_mask.astype(jnp.bfloat16)
    dispatch_wide = dispatch_mask.astype(jnp.float32)
    share_all = jnp.sum(jnp.where(selected, route_fixed, 0), axis=1).astype(jnp.float32) / 65536.0
    share = jnp.dot(dispatch_wide, share_all, precision=lax.Precision.HIGHEST)
    routed = jnp.sum(dispatch_wide, axis=1)
    picked = jnp.dot(dispatch, tokens, preferred_element_type=jnp.float32).astype(jnp.bfloat16)
    parts = lax.dynamic_update_index_in_dim(
        jnp.zeros((CAP, ntp, picked.shape[1]), jnp.bfloat16), picked, tensor_at, 1
    )
    for s in range(1, ntp):
        parts = lax.dynamic_update_index_in_dim(
            parts, shift_tensor(picked, s), (tensor_at + ntp - s) % ntp, 1
        )
    gathered = parts.reshape(CAP, -1)
    cot_rows = jnp.dot(dispatch, hidden_cot, preferred_element_type=jnp.float32).astype(
        jnp.bfloat16
    )

    depth = gathered.shape[1] // ndp
    features = gathered.reshape(CAP, n_high, 2, 2, 2 * depth)
    near = lax.dynamic_index_in_dim(features, z_low, 2, keepdims=False)
    far = flip(lax.dynamic_index_in_dim(features, 1 - z_low, 2, keepdims=False), 4)
    both = jnp.stack([near, far])
    here = lax.dynamic_index_in_dim(both, x_at, 3, keepdims=False)
    there = flip(lax.dynamic_index_in_dim(both, 1 - x_at, 3, keepdims=False), 2)
    mine = jnp.concatenate([here, there])
    group = jnp.stack([mine, flip(mine, 1)], axis=1)
    group = group.reshape(8 * CAP, n_high, 2, depth).transpose(1, 2, 3, 0)
    feats = jnp.stack(
        [
            lax.dynamic_index_in_dim(group, (z_high + s) % n_high, 0, keepdims=False)
            for s in range(n_high)
        ]
    )

    width = w_gate.shape[1]
    step = width // CHUNKS

    def cotangents(rows, chunk):
        columns = slice(chunk * (width // WIDE), (chunk + 1) * (width // WIDE))
        gate_pre = jnp.dot(rows, w_gate[:, columns], preferred_element_type=jnp.float32)
        up_pre = jnp.dot(rows, w_up[:, columns], preferred_element_type=jnp.float32)
        sigmoid_gate = jax.nn.sigmoid(gate_pre)
        activated = gate_pre * sigmoid_gate
        hidden = (activated * up_pre).astype(jnp.bfloat16)
        hidden = lax.optimization_barrier(hidden)
        cot_wide = cot_rows[:, columns].astype(jnp.float32)
        route = jnp.sum(hidden.astype(jnp.float32) * cot_wide, axis=1)
        scaled = share[:, None] * cot_wide
        gate_cot = (
            scaled * up_pre * sigmoid_gate * (1.0 + gate_pre * (1.0 - sigmoid_gate))
        ).astype(jnp.bfloat16)
        up_cot = (scaled * activated).astype(jnp.bfloat16)
        return gate_cot, up_cot, route

    kepts, passes, routes = [], [], []
    for chunk in range(WIDE):
        gate_cot, up_cot, route = cotangents(gathered, chunk)
        kept, passed = jnp.where(is_gate, gate_cot, up_cot), jnp.where(is_gate, up_cot, gate_cot)
        for part in range(CHUNKS // WIDE):
            kepts.append(kept[:, part * step : (part + 1) * step])
            passes.append(passed[:, part * step : (part + 1) * step])
        routes.append(route)
    route_sum = sum(routes)
    block = w_gate.shape[0] // ntp
    bf16, f32 = jnp.bfloat16, jnp.float32
    vmem = pl.BlockSpec(memory_space=pltpu.VMEM)
    anywhere = pl.BlockSpec(memory_space=pl.ANY)
    own, other, slot_grad = pl.pallas_call(
        functools.partial(exchange, ndp, ntp),
        out_shape=(
            jax.ShapeDtypeStruct((CHUNKS, depth, step), bf16),
            jax.ShapeDtypeStruct((CHUNKS, depth, step), bf16),
            jax.ShapeDtypeStruct((block, CAP), f32),
        ),
        in_specs=[vmem, vmem, vmem, anywhere, anywhere],
        out_specs=(vmem, vmem, vmem),
        scratch_shapes=[
            pltpu.VMEM((CHUNKS, 8 * CAP, step), bf16),
            pltpu.VMEM((n_high - 1, CHUNKS, 2, depth, step), bf16),
            pltpu.VMEM((n_high - 1, CHUNKS, 2, depth, step), bf16),
            pltpu.VMEM((CHUNKS, 2, depth, step), bf16),
            pltpu.VMEM((CHUNKS, depth, step), bf16),
            pltpu.VMEM((2, w_gate.shape[0], step), bf16),
            pltpu.VMEM((w_gate.shape[0], CAP), f32),
            pltpu.VMEM((ntp - 1, block, CAP), f32),
            pltpu.SemaphoreType.DMA((5, CHUNKS)),
            pltpu.SemaphoreType.DMA((5, CHUNKS)),
            pltpu.SemaphoreType.DMA((n_high - 1, CHUNKS)),
            pltpu.SemaphoreType.DMA((n_high - 1, CHUNKS)),
            pltpu.SemaphoreType.DMA((ntp - 1,)),
            pltpu.SemaphoreType.DMA((ntp - 1,)),
            pltpu.SemaphoreType.DMA((2,)),
        ],
        compiler_params=pltpu.CompilerParams(
            collective_id=0, has_side_effects=True, vmem_limit_bytes=58 * 2**20
        ),
        cost_estimate=pl.CostEstimate(
            flops=26 * 10**9, bytes_accessed=60 * 10**6, transcendentals=0
        ),
    )(jnp.stack(kepts), jnp.stack(passes), feats, w_gate, w_up)
    gate_grad = jnp.where(is_gate, own, other).transpose(1, 0, 2).reshape(depth, width)
    up_grad = jnp.where(is_gate, other, own).transpose(1, 0, 2).reshape(depth, width)

    slot_route = route_sum
    for s in range(1, ntp):
        slot_route += shift_tensor(route_sum, s)
    route_grad = jnp.dot(routed * slot_route, dispatch_wide, precision=lax.Precision.HIGHEST)

    back_dims = (((0,), (0,)), ((), ()))
    token_grad = lax.dot_general(
        dispatch,
        slot_grad.T.astype(jnp.bfloat16),
        back_dims,
        preferred_element_type=jnp.float32,
    ).astype(jnp.bfloat16)
    return token_grad, gate_grad, up_grad, route_grad


def solution(mesh):
    return jax.shard_map(
        functools.partial(on_device, mesh.shape["dp"], mesh.shape["tensor"]),
        mesh=mesh,
        in_specs=(
            P("dp", "tensor"),
            P("dp", "tensor"),
            P(None, "tensor"),
            P(None, "tensor"),
            P("dp", None),
            P("dp", None),
        ),
        out_specs=(P("dp", "tensor"), P("dp", "tensor"), P("dp", "tensor"), P("dp")),
        check_vma=False,
    )
```

```python
import functools

import jax
import jax.numpy as jnp
from jax import lax
from jax.experimental import pallas as pl
from jax.experimental.pallas import tpu as pltpu
from jax.sharding import PartitionSpec as P

CAP = 256
CHUNKS = 8
WIDE = 4
BY_Z = 3
MESH = pl.DeviceIdType.MESH


def exchange(ndp, ntp, feats, w_gate, w_up, *refs):
    kept_parts, passed_parts, refs = refs[:WIDE], refs[WIDE : 2 * WIDE], refs[2 * WIDE :]
    (own_out, other_out, slot_out, cots, partial, landed, summed, swapped, weights, grad, grad_in,
     send, recv, high_send, high_recv, y_send, y_recv, weight_sem) = refs
    n_high = ndp // 8
    me = lax.axis_index("dp")
    at = lax.axis_index("tensor")
    core, high = me % 2, me // 8
    core_peer = me + 1 - 2 * core
    x_peer = me + 2 - 4 * ((me // 2) % 2)
    z_peer = me + 4 - 8 * ((me // 4) % 2)
    highs = [((high + s) % n_high) * 8 + me % 8 for s in range(1, n_high)]
    tensors = [(at + s) % ntp for s in range(1, ntp)]
    slots, step = cots.shape[1] // 8, cots.shape[2]
    halves = CHUNKS // WIDE

    def kept(j):
        return kept_parts[j // halves].at[:, pl.ds(j % halves * step, step)]

    def passed(j):
        return passed_parts[j // halves].at[:, pl.ds(j % halves * step, step)]

    depth = own_out.shape[1]
    block = slot_out.shape[0]
    tile = min(block, 512)

    barrier = pltpu.get_barrier_semaphore()
    for peer in [core_peer, x_peer, z_peer] + highs:
        pl.semaphore_signal(barrier, inc=1, device_id=(peer, at), device_id_type=MESH)
    for peer in tensors:
        pl.semaphore_signal(barrier, inc=1, device_id=(me, peer), device_id_type=MESH)
    pl.semaphore_wait(barrier, 3 + len(highs) + len(tensors))

    def remote(src, dst, send_sem, recv_sem, device):
        return pltpu.make_async_remote_copy(
            src_ref=src, dst_ref=dst, send_sem=send_sem, recv_sem=recv_sem,
            device_id=device, device_id_type=MESH,
        )

    def rows(j, which, count=2):
        return cots.at[j, pl.ds(which * slots, count * slots)]

    def to_core(j):
        return remote(passed(j), rows(j, 1, 1), send.at[0, j], recv.at[0, j], (core_peer, at))

    def to_z(j):
        return remote(rows(j, 0), rows(j, 2), send.at[1, j], recv.at[1, j], (z_peer, at))

    def to_x(j):
        return remote(rows(j, 0), rows(j, 4), send.at[2, j], recv.at[2, j], (x_peer, at))

    def onward(j):
        if j == BY_Z:
            return remote(rows(j, 4), rows(j, 6), send.at[3, j], recv.at[3, j], (z_peer, at))
        return remote(rows(j, 2), rows(j, 6), send.at[3, j], recv.at[3, j], (x_peer, at))

    def swap(j):
        return remote(
            summed.at[j, 1 - core], swapped.at[j], send.at[4, j], recv.at[4, j], (core_peer, at)
        )

    def to_high(j, s):
        return remote(
            partial.at[s, j], landed.at[s, j], high_send.at[s, j], high_recv.at[s, j],
            (highs[s], at),
        )

    def to_tensor(s):
        start = pl.multiple_of(tensors[s] * block, block)
        return remote(
            grad.at[pl.ds(start, block)], grad_in.at[s], y_send.at[s], y_recv.at[s],
            (me, tensors[s]),
        )

    def weight_copy(i, source):
        columns = pl.ds((i // 2) * step, step)
        return pltpu.make_async_copy(
            source.at[:, columns], weights.at[i % 2], weight_sem.at[i % 2]
        )

    def fetch(i):
        takes_gate = core == i % 2

        @pl.when(takes_gate)
        def _():
            weight_copy(i, w_gate).start()

        @pl.when(jnp.logical_not(takes_gate))
        def _():
            weight_copy(i, w_up).start()

    def grad_turn(i):
        weight_copy(i, w_gate).wait()
        cot = (kept if i % 2 == 0 else passed)(i // 2)

        def body(k, carry):
            part = pl.ds(pl.multiple_of(k * tile, tile), tile)
            term = lax.dot_general(
                weights[i % 2, part, :], cot[...], (((1,), (1,)), ((), ())),
                preferred_element_type=jnp.float32,
            )
            grad[part, :] = term if i == 0 else grad[part, :] + term
            return carry

        lax.fori_loop(0, grad.shape[0] // tile, body, 0)
        if i + 2 < 2 * CHUNKS:
            fetch(i + 2)

    def multiply(j, s, half):
        return jnp.dot(feats[s, half], cots[j], preferred_element_type=jnp.float32)

    def send_sums(j):
        for s in range(n_high - 1):
            def body(half, carry):
                partial[s, j, half] = multiply(j, s + 1, half).astype(jnp.bfloat16)
                return carry

            lax.fori_loop(0, 2, body, 0)
            to_high(j, s).start()

    def finish(j):
        for s in range(n_high - 1):
            to_high(j, s).wait_recv()

        def body(half, carry):
            total = multiply(j, 0, half)
            for s in range(n_high - 1):
                total += landed[s, j, half].astype(jnp.float32)
            summed[j, half] = total.astype(jnp.bfloat16)
            return carry

        lax.fori_loop(0, 2, body, 0)
        swap(j).start()
        own_out[j] = summed[j, core]

    fetch(0)
    fetch(1)
    for j in range(CHUNKS):
        to_core(j).start()
    for j in range(CHUNKS):
        cots[j, 0:slots] = kept(j)[...]
    for t in range(CHUNKS + 2):
        if 1 <= t <= CHUNKS:
            (to_x if t - 1 == BY_Z else to_z)(t - 1).wait_recv()
            onward(t - 1).start()
        for j in range(0 if t == 0 else t + 1, min(t + 2, CHUNKS)):
            to_core(j).wait_recv()
            to_z(j).start()
            to_x(j).start()
        if t < CHUNKS:
            grad_turn(2 * t)
            grad_turn(2 * t + 1)
        if t == CHUNKS - 1:
            for s in range(ntp - 1):
                to_tensor(s).start()
        if t >= 2:
            (to_z if t - 2 == BY_Z else to_x)(t - 2).wait_recv()
            onward(t - 2).wait_recv()
            send_sums(t - 2)
        if t >= 4:
            finish(t - 4)
    for s in range(ntp - 1):
        to_tensor(s).wait_recv()
    here = pl.ds(pl.multiple_of(at * block, block), block)
    slot = grad[here, :]
    for s in range(ntp - 1):
        slot += grad_in[s]
    slot_out[...] = slot
    for j in range(CHUNKS - 2, CHUNKS):
        finish(j)
    for j in range(CHUNKS):
        swap(j).wait_recv()
        other_out[j] = swapped[j]
        for copy in (to_core(j), to_z(j), to_x(j), onward(j), swap(j)):
            copy.wait_send()
        for s in range(n_high - 1):
            to_high(j, s).wait_send()
    for s in range(ntp - 1):
        to_tensor(s).wait_send()


def on_device(ndp, ntp, tokens, hidden_cot, w_gate, w_up, expert_ids, route_fixed):
    n_high = ndp // 8
    me = lax.axis_index("dp")
    core, x_at, z_low, z_high = me % 2, (me // 2) % 2, (me // 4) % 2, me // 8
    tensor_at = lax.axis_index("tensor")
    is_gate = core == 0

    def flip(value, bit):
        return lax.ppermute(value, "dp", [(i, i ^ bit) for i in range(ndp)])

    def shift_high(value, step):
        return lax.ppermute(value, "dp", [(i, (i + 8 * step) % ndp) for i in range(ndp)])

    def shift_tensor(value, step):
        return lax.ppermute(value, "tensor", [(i, (i + step) % ntp) for i in range(ntp)])

    selected = expert_ids == 0
    routed_flag = jnp.any(selected, axis=1)
    slot_of = jnp.cumsum(routed_flag.astype(jnp.int32)) - 1
    slot_ids = jnp.arange(CAP, dtype=jnp.int32)
    dispatch_mask = (slot_of[None, :] == slot_ids[:, None]) & routed_flag[None, :]
    dispatch = dispatch_mask.astype(jnp.bfloat16)
    dispatch_wide = dispatch_mask.astype(jnp.float32)
    share_all = jnp.sum(jnp.where(selected, route_fixed, 0), axis=1).astype(jnp.float32) / 65536.0
    share = jnp.dot(dispatch_wide, share_all, precision=lax.Precision.HIGHEST)
    routed = jnp.sum(dispatch_wide, axis=1)
    picked = jnp.dot(dispatch, tokens, preferred_element_type=jnp.float32).astype(jnp.bfloat16)
    parts = lax.dynamic_update_index_in_dim(
        jnp.zeros((CAP, ntp, picked.shape[1]), jnp.bfloat16), picked, tensor_at, 1
    )
    for s in range(1, ntp):
        parts = lax.dynamic_update_index_in_dim(
            parts, shift_tensor(picked, s), (tensor_at + ntp - s) % ntp, 1
        )
    gathered = parts.reshape(CAP, -1)
    cot_rows = jnp.dot(dispatch, hidden_cot, preferred_element_type=jnp.float32).astype(
        jnp.bfloat16
    )

    depth = gathered.shape[1] // ndp
    features = gathered.reshape(CAP, n_high, 2, 2, 2 * depth)
    near = lax.dynamic_index_in_dim(features, z_low, 2, keepdims=False)
    far = flip(lax.dynamic_index_in_dim(features, 1 - z_low, 2, keepdims=False), 4)

    def cross(far):
        both = jnp.stack([near, far])
        here = lax.dynamic_index_in_dim(both, x_at, 3, keepdims=False)
        return here, flip(lax.dynamic_index_in_dim(both, 1 - x_at, 3, keepdims=False), 2)

    width = w_gate.shape[1]
    step = width // CHUNKS

    def cotangents(rows, chunk):
        columns = slice(chunk * (width // WIDE), (chunk + 1) * (width // WIDE))
        gate_pre = jnp.dot(rows, w_gate[:, columns], preferred_element_type=jnp.float32)
        up_pre = jnp.dot(rows, w_up[:, columns], preferred_element_type=jnp.float32)
        sigmoid_gate = jax.nn.sigmoid(gate_pre)
        activated = gate_pre * sigmoid_gate
        hidden = (activated * up_pre).astype(jnp.bfloat16)
        hidden = lax.optimization_barrier(hidden)
        cot_wide = cot_rows[:, columns].astype(jnp.float32)
        route = jnp.sum(hidden.astype(jnp.float32) * cot_wide, axis=1)
        scaled = share[:, None] * cot_wide
        gate_cot = (
            scaled * up_pre * sigmoid_gate * (1.0 + gate_pre * (1.0 - sigmoid_gate))
        ).astype(jnp.bfloat16)
        up_cot = (scaled * activated).astype(jnp.bfloat16)
        return gate_cot, up_cot, route

    kepts, passes, routes = [], [], []
    tied = gathered
    for chunk in range(WIDE):
        if chunk == 2:
            tied, far = lax.optimization_barrier((tied, far))
            here, there = cross(far)
        if chunk == 3:
            tied, there = lax.optimization_barrier((tied, there))
        gate_cot, up_cot, route = cotangents(tied, chunk)
        kepts.append(jnp.where(is_gate, gate_cot, up_cot))
        passes.append(jnp.where(is_gate, up_cot, gate_cot))
        routes.append(route)
    mine = jnp.concatenate([here, there])
    group = jnp.stack([mine, flip(mine, 1)], axis=1)
    group = group.reshape(8 * CAP, n_high, 2, depth).transpose(1, 2, 3, 0)
    feats = jnp.stack(
        [
            lax.dynamic_index_in_dim(group, (z_high + s) % n_high, 0, keepdims=False)
            for s in range(n_high)
        ]
    )
    route_sum = sum(routes)
    block = w_gate.shape[0] // ntp
    bf16, f32 = jnp.bfloat16, jnp.float32
    vmem = pl.BlockSpec(memory_space=pltpu.VMEM)
    anywhere = pl.BlockSpec(memory_space=pl.ANY)
    own, other, slot_grad = pl.pallas_call(
        functools.partial(exchange, ndp, ntp),
        out_shape=(
            jax.ShapeDtypeStruct((CHUNKS, depth, step), bf16),
            jax.ShapeDtypeStruct((CHUNKS, depth, step), bf16),
            jax.ShapeDtypeStruct((block, CAP), f32),
        ),
        in_specs=[vmem, anywhere, anywhere] + [vmem] * (2 * WIDE),
        out_specs=(vmem, vmem, vmem),
        scratch_shapes=[
            pltpu.VMEM((CHUNKS, 8 * CAP, step), bf16),
            pltpu.VMEM((n_high - 1, CHUNKS, 2, depth, step), bf16),
            pltpu.VMEM((n_high - 1, CHUNKS, 2, depth, step), bf16),
            pltpu.VMEM((CHUNKS, 2, depth, step), bf16),
            pltpu.VMEM((CHUNKS, depth, step), bf16),
            pltpu.VMEM((2, w_gate.shape[0], step), bf16),
            pltpu.VMEM((w_gate.shape[0], CAP), f32),
            pltpu.VMEM((ntp - 1, block, CAP), f32),
            pltpu.SemaphoreType.DMA((5, CHUNKS)),
            pltpu.SemaphoreType.DMA((5, CHUNKS)),
            pltpu.SemaphoreType.DMA((n_high - 1, CHUNKS)),
            pltpu.SemaphoreType.DMA((n_high - 1, CHUNKS)),
            pltpu.SemaphoreType.DMA((ntp - 1,)),
            pltpu.SemaphoreType.DMA((ntp - 1,)),
            pltpu.SemaphoreType.DMA((2,)),
        ],
        compiler_params=pltpu.CompilerParams(
            collective_id=0, has_side_effects=True, vmem_limit_bytes=58 * 2**20
        ),
        cost_estimate=pl.CostEstimate(
            flops=26 * 10**9, bytes_accessed=60 * 10**6, transcendentals=0
        ),
    )(feats, w_gate, w_up, *kepts, *passes)
    gate_grad = jnp.where(is_gate, own, other).transpose(1, 0, 2).reshape(depth, width)
    up_grad = jnp.where(is_gate, other, own).transpose(1, 0, 2).reshape(depth, width)

    slot_route = route_sum
    for s in range(1, ntp):
        slot_route += shift_tensor(route_sum, s)
    route_grad = jnp.dot(routed * slot_route, dispatch_wide, precision=lax.Precision.HIGHEST)

    back_dims = (((0,), (0,)), ((), ()))
    token_grad = lax.dot_general(
        dispatch,
        slot_grad.T.astype(jnp.bfloat16),
        back_dims,
        preferred_element_type=jnp.float32,
    ).astype(jnp.bfloat16)
    return token_grad, gate_grad, up_grad, route_grad


def solution(mesh):
    return jax.shard_map(
        functools.partial(on_device, mesh.shape["dp"], mesh.shape["tensor"]),
        mesh=mesh,
        in_specs=(
            P("dp", "tensor"),
            P("dp", "tensor"),
            P(None, "tensor"),
            P(None, "tensor"),
            P("dp", None),
            P("dp", None),
        ),
        out_specs=(P("dp", "tensor"), P("dp", "tensor"), P("dp", "tensor"), P("dp")),
        check_vma=False,
    )
```
